32 devices in a mesh: req: 16 (over z, y, core), tp: 2 (over x).
Axes of the slice: x: 2, y: 2, z: 4, core: 2. Of those that a mesh axis runs over, the one named last changes fastest.
Arguments:
- text_stream: bfloat16 [16384, 4096], P('req', 'tp'), may hold values from -6 to 6
- image_rows: bfloat16 [8192, 4096], P('req', 'tp'), may hold values from -8 to 8
- positions: int32 [8192], P('req'), may hold values from 0 to 16383, as said below
- norm_gain: bfloat16 [4096], P('tp'), may hold values from 0.099609375 to 1.8984375
- kv_weight: bfloat16 [4096, 2048], P('tp'), may hold values from -0.125 to 0.125
Outputs:
- key_value: bfloat16 [2048, 16384], P('tp', 'req')
The draws below stay inside these ranges and needn't reach their ends.
Inputs may be any that keep to these rules, and one draw needn't show every extreme that they name: All entries of positions are distinct. Among the image rows of one index of req, at most 64 have positions in the stream rows of any one index of req, and in every draw some index of req receives exactly that many from every index.
All inputs are finite; a program needn't handle non-finite values.
Results may differ from the reference program's by a relative error of at most 0.008.
Values may be sent and summed in bfloat16 or wider, within the bound.
A program may use at most 64 MiB of HBM per device.

```python
import jax
import jax.numpy as jnp
from jax import lax

D = 4096
ROWS_DEV = 1024
IMG_DEV = 512
KV_COLS = 2048
STREAM = 16384
IMAGES = 8192
N_REQ = 16
N_TP = 2


def draw_positions(key, part):
    most = ROWS_DEV // N_REQ
    blocks = IMG_DEV
    slots_all = N_REQ * most
    key_full = jax.random.fold_in(key, 11)
    key_perm = jax.random.fold_in(key, 12)
    key_assign = jax.random.fold_in(key, 13)
    key_offset = jax.random.fold_in(key, 14)
    full_owner = jax.random.randint(key_full, (), 0, N_REQ)
    own_slots = full_owner * most + jnp.arange(most, dtype=jnp.int32)
    sources = jnp.arange(N_REQ, dtype=jnp.int32)

    def pick_slots(source):
        others = jax.random.permutation(jax.random.fold_in(key_perm, source), slots_all).astype(jnp.int32)
        is_own = (others // most == full_owner).astype(jnp.int32)
        ordered = others[jnp.argsort(is_own, stable=True)]
        chosen = jnp.concatenate([own_slots, ordered[:blocks - most]])
        return jax.random.permutation(jax.random.fold_in(key_assign, source), chosen).astype(jnp.int32)
    chosen_all = jax.vmap(pick_slots)(sources)

    def owner_offsets(owner):
        return jax.random.permutation(jax.random.fold_in(key_offset, owner), ROWS_DEV).astype(jnp.int32)
    offset_tables = jax.vmap(owner_offsets)(sources)
    owners = chosen_all // most
    within = chosen_all % most
    slot_index = within * N_REQ + sources[:, None]
    local = offset_tables[owners, slot_index]
    table = owners * ROWS_DEV + local
    return table.reshape(-1).astype(jnp.int32)


def strengthened(array, stream_key, source, target, parts, factor):
    def block_of(axis_at):
        return (jnp.arange(array.shape[axis_at]) // (array.shape[axis_at] // parts)).reshape((-1,) + (1,) * (array.ndim - 1 - axis_at))

    first = jax.random.permutation(stream_key, parts)[block_of(target)]
    other_side = (block_of(target) + parts // 2) % parts
    return jnp.where((block_of(source) == first) | (block_of(source) == other_side), factor * array, array)


def levels(own_key, shape, cuts, low, high):
    gain = 1.0
    for axis_at, shards_of in cuts:
        draws = jax.random.uniform(jax.random.fold_in(jax.random.fold_in(own_key, 6), axis_at), (shards_of,), jnp.float32, low / len(cuts), high / len(cuts))
        gain = gain * jnp.repeat(jnp.exp(draws), shape[axis_at] // shards_of).reshape((-1,) + (1,) * (len(shape) - 1 - axis_at))
    return gain


def normal_values(key, shape, deviation, bound, shards=(), kind=jnp.bfloat16):
    result = deviation * jax.random.normal(key, shape, jnp.float32)
    if shards:
        result = result * levels(key, shape, shards, -0.22, 0.18)
    return jnp.clip(result, -bound, bound).astype(kind)


def heavy_noise(key, extent, spread, reach, pieces, heavy, held_as=jnp.bfloat16):
    drawn = spread * jax.random.normal(key, extent, jnp.float32)
    if pieces:
        drawn = drawn * levels(key, extent, pieces, -0.22, 0.18)
    return jnp.clip(strengthened(drawn, jax.random.fold_in(key, 3), *heavy), -reach, reach).astype(held_as)


def setup_inputs(seed: int = 0) -> dict:
    key_of = jax.random.split(jax.random.key(seed), 6)
    return {
        "text_stream": normal_values(key_of[0], (STREAM, D), 1.0, 6.0, ((0, 16), (1, 2))),
        "image_rows": normal_values(key_of[1], (IMAGES, D), 1.5, 8.0, ((0, 16), (1, 2))),
        "positions": draw_positions(jax.random.fold_in(key_of[5], 71), 0),
        "norm_gain": jnp.clip(1.0 + 0.18 * jax.random.normal(key_of[3], (D,), jnp.float32), 0.099609375, 1.8984375).astype(jnp.bfloat16),
        "kv_weight": heavy_noise(key_of[4], (D, KV_COLS), D ** -0.5, 0.125, ((0, 2),), (0, 1, 2, 2.0)),
    }


EPSILON = 1e-05

def reference(text_stream, image_rows, positions, norm_gain, kv_weight):
    merged = text_stream.at[positions].set(image_rows)
    totals = lax.optimization_barrier(jnp.sum(jnp.square(merged.astype(jnp.float32)), axis=1))
    inverse = lax.rsqrt(totals / D + EPSILON)
    normed = (merged.astype(jnp.float32) * inverse[:, None] * norm_gain.astype(jnp.float32)[None, :]).astype(jnp.bfloat16)
    group = D // N_TP
    summed = jnp.zeros((KV_COLS, STREAM), jnp.float32)
    for index in range(N_TP):
        part_term = lax.dot_general(kv_weight[index * group:(index + 1) * group], normed[:, index * group:(index + 1) * group], (((0,), (1,)), ((), ())), preferred_element_type=jnp.float32)
        rounded = lax.optimization_barrier(part_term.astype(jnp.bfloat16))
        summed = summed + rounded.astype(jnp.float32)
    return summed.astype(jnp.bfloat16)
```

```python
import functools

import jax
import jax.numpy as jnp
from jax import lax
from jax.experimental import pallas as pl
from jax.experimental.pallas import tpu as pltpu
from jax.sharding import PartitionSpec as P

EPSILON = 1e-05
LANES = 128
CHUNKS = 4
MESH = pl.DeviceIdType.MESH
F32 = jnp.float32
BF16 = jnp.bfloat16


def iota(shape, dim):
    return lax.broadcasted_iota(jnp.int32, shape, dim)


def loop(start, stop, body):
    def step(i, carry):
        body(i)
        return carry

    lax.fori_loop(start, stop, step, 0)


def square_and_gain(x_ref, gain_ref, squares_ref):
    gain = gain_ref[...].astype(F32)

    def body(b):
        rows = pl.ds(pl.multiple_of(b * LANES, LANES), LANES)
        x = x_ref[rows, :].astype(F32)
        total = jnp.zeros((LANES, LANES), F32)
        for k in range(x.shape[1] // LANES):
            piece = x[:, k * LANES:(k + 1) * LANES]
            total = total + piece * piece
        squares_ref[b] = jnp.sum(total.T, axis=0, keepdims=True)
        x_ref[rows, :] = (x * gain).astype(BF16)

    loop(0, x_ref.shape[0] // LANES, body)


def kernel(
    n, width, pos_ref, gain_ref, img_hbm, text_hbm, w_hbm, out_hbm,
    img, text, w, pos_all, rank, p_send, p_recv, p_own, t_send, t_recv, t_own,
    sq_img, sq_img_in, sq_text, sq_text_in, inv_img, pick, pack, arrived, place, outv,
    ld_sem, w_sem, pos_s, pos_r, sq_s, sq_r, p_s, p_r, t_s, t_r, a_s, a_r, o_sem,
):
    req, tp = lax.axis_index("req"), lax.axis_index("tp")
    peer = 1 - tp
    images, rows = img.shape[0], text.shape[0]
    cw = w.shape[3]
    half = CHUNKS * cw
    slots = place.shape[0]
    cap = slots // n

    def other(i):
        return lax.rem(req + i, n)

    def load_w(side, owner, c):
        return pltpu.make_async_copy(
            w_hbm.at[:, pl.ds(pl.multiple_of(owner * half + c * cw, cw), cw)], w.at[side, c], w_sem.at[side, c]
        )

    load_img = pltpu.make_async_copy(img_hbm, img, ld_sem.at[0])
    load_text = pltpu.make_async_copy(text_hbm, text, ld_sem.at[1])
    load_img.start()
    loop(0, CHUNKS, lambda c: load_w(0, peer, c).start())
    load_text.start()
    loop(0, CHUNKS, lambda c: load_w(1, tp, c).start())

    barrier = pltpu.get_barrier_semaphore()
    loop(1, n, lambda i: pl.semaphore_signal(barrier, inc=1, device_id={"req": other(i)}, device_id_type=MESH))
    pl.semaphore_signal(barrier, inc=1, device_id={"tp": peer}, device_id_type=MESH)
    pl.semaphore_wait(barrier, n)

    def across(src, dst, send, recv):
        return pltpu.make_async_remote_copy(
            src_ref=src, dst_ref=dst, send_sem=send, recv_sem=recv, device_id={"tp": peer}, device_id_type=MESH
        )

    def pos_copy(i, source):
        return pltpu.make_async_remote_copy(
            src_ref=pos_all.at[source], dst_ref=pos_all.at[source], send_sem=pos_s.at[i],
            recv_sem=pos_r.at[source], device_id={"req": other(i)}, device_id_type=MESH,
        )

    pos_all[pl.ds(req, 1)] = pos_ref[...].reshape(1, 1, images)
    loop(1, n, lambda i: pos_copy(i, req).start())

    load_img.wait()
    square_and_gain(img, gain_ref, sq_img)
    copy_sq_img = across(sq_img, sq_img_in, sq_s.at[0], sq_r.at[0])
    copy_sq_img.start()

    def p_copy(c):
        return across(p_send.at[c], p_recv.at[c], p_s.at[c], p_r.at[c])

    def image_send(c):
        load_w(0, peer, c).wait()
        p_send[c] = jnp.dot(img[...], w[0, c], preferred_element_type=F32).astype(BF16)
        p_copy(c).start()

    loop(0, CHUNKS, image_send)

    row_pos = pos_ref[...]
    dest = iota((n, images), 0)
    member = (row_pos >= dest * rows) & (row_pos < (dest + 1) * rows)
    earlier = (iota((images, images), 0) < iota((images, images), 1)).astype(F32).astype(BF16)
    ones = member.astype(F32)
    before = jnp.dot(ones.astype(BF16), earlier, preferred_element_type=F32)
    target = jnp.sum((before + (dest * cap).astype(F32)) * ones, axis=0, keepdims=True)
    slot = iota((slots, images), 0).astype(F32)
    pick[...] = (slot == target).astype(F32).astype(BF16)

    load_text.wait()
    square_and_gain(text, gain_ref, sq_text)

    def t_copy(c):
        return across(t_send.at[c], t_recv.at[c], t_s.at[c], t_r.at[c])

    def text_send(c):
        t_send[c] = jnp.dot(text[...], w[0, c], preferred_element_type=F32).astype(BF16)

    text_send(0)

    def image_own(c):
        load_w(1, tp, c).wait()
        p_own[c] = jnp.dot(img[...], w[1, c], preferred_element_type=F32)

    loop(0, CHUNKS, image_own)

    copy_sq_img.wait()

    def inv_body(b):
        inv = lax.rsqrt((sq_img[b] + sq_img_in[b]) / width + EPSILON)
        inv_img[pl.ds(pl.multiple_of(b * LANES, LANES), LANES), :] = jnp.broadcast_to(inv, (LANES, LANES)).T

    loop(0, images // LANES, inv_body)

    def a_copy(c, i, dst, source):
        return pltpu.make_async_remote_copy(
            src_ref=pack.at[c, pl.ds(pl.multiple_of(dst * cap, cap), cap), :],
            dst_ref=arrived.at[c, pl.ds(pl.multiple_of(source * cap, cap), cap), :],
            send_sem=a_s.at[c, i], recv_sem=a_r.at[c, source],
            device_id={"req": other(i)}, device_id_type=MESH,
        )

    copy_sq_text = across(sq_text, sq_text_in, sq_s.at[1], sq_r.at[1])
    copy_sq_text.start()

    def image_pack(c):
        p_copy(c).wait_recv()
        t_copy(c).start()
        total = p_own[c] + p_recv[c].astype(F32)
        inv = inv_img[...]
        y = jnp.concatenate(
            [total[:, k * LANES:(k + 1) * LANES] * inv for k in range(cw // LANES)], axis=1
        ).astype(BF16)
        pack[c] = jnp.dot(pick[...], y, preferred_element_type=F32).astype(BF16)
        loop(1, n, lambda i: a_copy(c, i, other(i), req).start())
        mine = pl.ds(pl.multiple_of(req * cap, cap), cap)
        arrived[c, mine, :] = pack[c, mine, :]

        @pl.when(c + 1 < CHUNKS)
        def _():
            text_send(c + 1)

    loop(0, CHUNKS, image_pack)

    loop(1, n, lambda i: pos_copy(i, other(i)).wait_recv())
    all_pos = pos_all[:, 0, :]
    local = all_pos - req * rows
    here = (local >= 0) & (local < rows)
    here_f = here.astype(F32)
    order = jnp.dot(here_f.astype(BF16), earlier, preferred_element_type=F32)
    rank[0] = jnp.where(here, order, -1.0)
    rank[1] = local.astype(F32) + 1.0

    def place_body(g):
        eight = pl.ds(pl.multiple_of(g * 8, 8), 8)
        order8 = rank[0, eight, :]
        local8 = rank[1, eight, :]
        for k in range(8):
            hit = iota((cap, images), 0).astype(F32) == order8[k:k + 1, :]
            at = jnp.sum(jnp.where(hit, local8[k:k + 1, :], 0.0), axis=1, keepdims=True)
            block = (iota((cap, rows), 1).astype(F32) + 1.0) == at
            place[pl.ds(pl.multiple_of((g * 8 + k) * cap, cap), cap), :] = block.astype(F32).astype(BF16)

    loop(0, n // 8, place_body)

    def text_own(c):
        t_own[c] = jnp.dot(text[...], w[1, c], preferred_element_type=F32)

    loop(0, CHUNKS, text_own)
    filled = jnp.max(place[...].astype(F32), axis=0, keepdims=True)
    copy_sq_text.wait()

    def out_copy(c):
        return pltpu.make_async_copy(
            outv.at[c], out_hbm.at[pl.ds(pl.multiple_of(c * cw, cw), cw), :], o_sem.at[c]
        )

    def finish(c):
        loop(1, n, lambda i: a_copy(c, i, req, other(i)).wait_recv())
        images_t = jnp.dot(arrived[c].T, place[...], preferred_element_type=F32)
        t_copy(c).wait_recv()
        for b in range(rows // LANES):
            at = slice(b * LANES, (b + 1) * LANES)
            inv = lax.rsqrt((sq_text[b] + sq_text_in[b]) / width + EPSILON)
            texts = (t_own[c, at, :] + t_recv[c, at, :].astype(F32)).T * inv
            outv[c, :, at] = jnp.where(filled[:, at] > 0.5, images_t[:, at], texts).astype(BF16)
        out_copy(c).start()

    loop(0, CHUNKS, finish)

    loop(1, n, lambda i: pos_copy(i, req).wait_send())

    def drain(c):
        p_copy(c).wait_send()
        t_copy(c).wait_send()
        loop(1, n, lambda i: a_copy(c, i, other(i), req).wait_send())
        out_copy(c).wait()

    loop(0, CHUNKS, drain)


def local(text_stream, image_rows, positions, norm_gain, kv_weight):
    n, sides = lax.axis_size("req"), lax.axis_size("tp")
    rows, features = text_stream.shape
    images = image_rows.shape[0]
    half = kv_weight.shape[1] // sides
    cw = half // CHUNKS
    slots = 2 * images
    any_spec, vmem = pl.BlockSpec(memory_space=pl.ANY), pl.BlockSpec(memory_space=pltpu.VMEM)
    dma = pltpu.SemaphoreType.DMA
    return pl.pallas_call(
        functools.partial(kernel, n, features * sides),
        out_shape=jax.ShapeDtypeStruct((half, rows), BF16),
        in_specs=[vmem, vmem, any_spec, any_spec, any_spec],
        out_specs=any_spec,
        scratch_shapes=[
            pltpu.VMEM((images, features), BF16),
            pltpu.VMEM((rows, features), BF16),
            pltpu.VMEM((2, CHUNKS, features, cw), BF16),
            pltpu.VMEM((n, 1, images), jnp.int32),
            pltpu.VMEM((2, n, images), F32),
            pltpu.VMEM((CHUNKS, images, cw), BF16),
            pltpu.VMEM((CHUNKS, images, cw), BF16),
            pltpu.VMEM((CHUNKS, images, cw), F32),
            pltpu.VMEM((CHUNKS, rows, cw), BF16),
            pltpu.VMEM((CHUNKS, rows, cw), BF16),
            pltpu.VMEM((CHUNKS, rows, cw), F32),
            pltpu.VMEM((images // LANES, 1, LANES), F32),
            pltpu.VMEM((images // LANES, 1, LANES), F32),
            pltpu.VMEM((rows // LANES, 1, LANES), F32),
            pltpu.VMEM((rows // LANES, 1, LANES), F32),
            pltpu.VMEM((images, LANES), F32),
            pltpu.VMEM((slots, images), BF16),
            pltpu.VMEM((CHUNKS, slots, cw), BF16),
            pltpu.VMEM((CHUNKS, slots, cw), BF16),
            pltpu.VMEM((slots, rows), BF16),
            pltpu.VMEM((CHUNKS, cw, rows), BF16),
            dma((2,)), dma((2, CHUNKS)), dma((n,)), dma((n,)), dma((2,)), dma((2,)),
            dma((CHUNKS,)), dma((CHUNKS,)), dma((CHUNKS,)), dma((CHUNKS,)),
            dma((CHUNKS, n)), dma((CHUNKS, n)), dma((CHUNKS,)),
        ],
        compiler_params=pltpu.CompilerParams(
            collective_id=0, has_side_effects=True, vmem_limit_bytes=56 * 1024 * 1024
        ),
        cost_estimate=pl.CostEstimate(
            flops=2 * (rows + images) * features * half * sides, bytes_accessed=16 << 20, transcendentals=0
        ),
    )(
        positions.reshape(1, images), norm_gain.reshape(1, features),
        image_rows, text_stream, kv_weight,
    )


def solution(mesh):
    return jax.shard_map(
        local,
        mesh=mesh,
        in_specs=(P("req", "tp"), P("req", "tp"), P("req"), P("tp"), P("tp", None)),
        out_specs=P("tp", "req"),
        check_vma=False,
    )
```

```python
import functools

import jax
import jax.numpy as jnp
from jax import lax
from jax.experimental import pallas as pl
from jax.experimental.pallas import tpu as pltpu
from jax.sharding import PartitionSpec as P

EPSILON = 1e-05
LANES = 128
CHUNKS = 4
LATE = 1
EARLY = CHUNKS - LATE
MESH = pl.DeviceIdType.MESH
F32 = jnp.float32
BF16 = jnp.bfloat16


def iota(shape, dim):
    return lax.broadcasted_iota(jnp.int32, shape, dim)


def loop(start, stop, body):
    def step(i, carry):
        body(i)
        return carry

    lax.fori_loop(start, stop, step, 0)


def square_and_gain(x_ref, gain_ref, squares_ref):
    gain = gain_ref[...].astype(F32)

    def body(b):
        rows = pl.ds(pl.multiple_of(b * LANES, LANES), LANES)
        x = x_ref[rows, :].astype(F32)
        total = jnp.zeros((LANES, LANES), F32)
        for k in range(x.shape[1] // LANES):
            piece = x[:, k * LANES:(k + 1) * LANES]
            total = total + piece * piece
        squares_ref[b] = jnp.sum(total.T, axis=0, keepdims=True)
        x_ref[rows, :] = (x * gain).astype(BF16)

    loop(0, x_ref.shape[0] // LANES, body)


def kernel(
    n, width, pos_ref, gain_ref, img_hbm, text_hbm, w_hbm, out_hbm,
    img, text, w, pos_all, rank, p_send, p_recv, p_own, t_send, t_recv, t_own,
    u_send, u_recv, u_own,
    sq_img, sq_img_in, sq_text, sq_text_in, inv_img, pick, pack, arrived, place, outv,
    ld_sem, w_sem, pos_s, pos_r, sq_s, sq_r, p_s, p_r, t_s, t_r, u_s, u_r, a_s, a_r, o_sem,
):
    req, tp = lax.axis_index("req"), lax.axis_index("tp")
    peer = 1 - tp
    images, rows = img.shape[0], text.shape[0]
    cw = w.shape[3]
    half = CHUNKS * cw
    slots = place.shape[0]
    cap = slots // n

    def other(i):
        return lax.rem(req + i, n)

    def load_w(side, owner, c):
        return pltpu.make_async_copy(
            w_hbm.at[:, pl.ds(pl.multiple_of(owner * half + c * cw, cw), cw)], w.at[side, c], w_sem.at[side, c]
        )

    load_img = pltpu.make_async_copy(img_hbm, img, ld_sem.at[0])
    load_text = pltpu.make_async_copy(text_hbm, text, ld_sem.at[1])
    load_img.start()
    loop(0, CHUNKS, lambda c: load_w(0, peer, c).start())
    loop(EARLY, CHUNKS, lambda c: load_w(1, tp, c).start())
    load_text.start()
    loop(0, EARLY, lambda c: load_w(1, tp, c).start())

    barrier = pltpu.get_barrier_semaphore()
    loop(1, n, lambda i: pl.semaphore_signal(barrier, inc=1, device_id={"req": other(i)}, device_id_type=MESH))
    pl.semaphore_signal(barrier, inc=1, device_id={"tp": peer}, device_id_type=MESH)
    pl.semaphore_wait(barrier, n)

    def across(src, dst, send, recv):
        return pltpu.make_async_remote_copy(
            src_ref=src, dst_ref=dst, send_sem=send, recv_sem=recv, device_id={"tp": peer}, device_id_type=MESH
        )

    def pos_copy(i, source):
        return pltpu.make_async_remote_copy(
            src_ref=pos_all.at[source], dst_ref=pos_all.at[source], send_sem=pos_s.at[i],
            recv_sem=pos_r.at[source], device_id={"req": other(i)}, device_id_type=MESH,
        )

    pos_all[pl.ds(req, 1)] = pos_ref[...].reshape(1, 1, images)
    loop(1, n, lambda i: pos_copy(i, req).start())

    load_img.wait()
    square_and_gain(img, gain_ref, sq_img)
    copy_sq_img = across(sq_img, sq_img_in, sq_s.at[0], sq_r.at[0])
    copy_sq_img.start()

    def p_copy(c):
        return across(p_send.at[c], p_recv.at[c], p_s.at[c], p_r.at[c])

    def image_send(c):
        load_w(0, peer, c).wait()
        p_send[c] = jnp.dot(img[...], w[0, c], preferred_element_type=F32).astype(BF16)
        p_copy(c).start()

    loop(0, EARLY, image_send)

    row_pos = pos_ref[...]
    dest = iota((n, images), 0)
    member = (row_pos >= dest * rows) & (row_pos < (dest + 1) * rows)
    earlier = (iota((images, images), 0) < iota((images, images), 1)).astype(F32).astype(BF16)
    ones = member.astype(F32)
    before = jnp.dot(ones.astype(BF16), earlier, preferred_element_type=F32)
    target = jnp.sum((before + (dest * cap).astype(F32)) * ones, axis=0, keepdims=True)
    slot = iota((slots, images), 0).astype(F32)
    pick[...] = (slot == target).astype(F32).astype(BF16)

    copy_sq_img.wait()

    def inv_body(b):
        inv = lax.rsqrt((sq_img[b] + sq_img_in[b]) / width + EPSILON)
        inv_img[pl.ds(pl.multiple_of(b * LANES, LANES), LANES), :] = jnp.broadcast_to(inv, (LANES, LANES)).T

    loop(0, images // LANES, inv_body)

    def a_copy(c, i, dst, source):
        return pltpu.make_async_remote_copy(
            src_ref=pack.at[c, pl.ds(pl.multiple_of(dst * cap, cap), cap), :],
            dst_ref=arrived.at[c, pl.ds(pl.multiple_of(source * cap, cap), cap), :],
            send_sem=a_s.at[c, i], recv_sem=a_r.at[c, source],
            device_id={"req": other(i)}, device_id_type=MESH,
        )

    def pack_and_send(k, scaled):
        pack[k] = jnp.dot(pick[...], scaled, preferred_element_type=F32).astype(BF16)
        loop(1, n, lambda i: a_copy(k, i, other(i), req).start())
        mine = pl.ds(pl.multiple_of(req * cap, cap), cap)
        arrived[k, mine, :] = pack[k, mine, :]

    def scale(total):
        inv = inv_img[...]
        return jnp.concatenate(
            [total[:, k * LANES:(k + 1) * LANES] * inv for k in range(cw // LANES)], axis=1
        ).astype(BF16)

    def image_late(c):
        for side, owner, k in ((0, peer, CHUNKS - EARLY + c), (1, tp, c)):
            load_w(side, owner, c).wait()
            pack_and_send(k, scale(jnp.dot(img[...], w[side, c], preferred_element_type=F32)))

    loop(EARLY, CHUNKS, image_late)

    load_text.wait()
    square_and_gain(text, gain_ref, sq_text)

    def t_copy(c):
        return across(t_send.at[c], t_recv.at[c], t_s.at[c], t_r.at[c])

    def text_send(c):
        t_send[c] = jnp.dot(text[...], w[0, c], preferred_element_type=F32).astype(BF16)

    text_send(0)

    def image_own(c):
        load_w(1, tp, c).wait()
        p_own[c] = jnp.dot(img[...], w[1, c], preferred_element_type=F32)

    loop(0, EARLY, image_own)

    copy_sq_text = across(sq_text, sq_text_in, sq_s.at[1], sq_r.at[1])
    copy_sq_text.start()

    def image_pack(c):
        p_copy(c).wait_recv()
        t_copy(c).start()
        pack_and_send(c, scale(p_own[c] + p_recv[c].astype(F32)))

        @pl.when(c + 1 < EARLY)
        def _():
            text_send(c + 1)

    loop(0, EARLY, image_pack)

    loop(1, n, lambda i: pos_copy(i, other(i)).wait_recv())
    all_pos = pos_all[:, 0, :]
    local = all_pos - req * rows
    here = (local >= 0) & (local < rows)
    here_f = here.astype(F32)
    order = jnp.dot(here_f.astype(BF16), earlier, preferred_element_type=F32)
    rank[0] = jnp.where(here, order, -1.0)
    rank[1] = local.astype(F32) + 1.0

    def place_body(g):
        eight = pl.ds(pl.multiple_of(g * 8, 8), 8)
        order8 = rank[0, eight, :]
        local8 = rank[1, eight, :]
        for k in range(8):
            hit = iota((cap, images), 0).astype(F32) == order8[k:k + 1, :]
            at = jnp.sum(jnp.where(hit, local8[k:k + 1, :], 0.0), axis=1, keepdims=True)
            block = (iota((cap, rows), 1).astype(F32) + 1.0) == at
            place[pl.ds(pl.multiple_of((g * 8 + k) * cap, cap), cap), :] = block.astype(F32).astype(BF16)

    loop(0, n // 8, place_body)

    def text_own(c):
        t_own[c] = jnp.dot(text[...], w[1, c], preferred_element_type=F32)

    loop(0, CHUNKS, text_own)
    filled = jnp.max(place[...].astype(F32), axis=0, keepdims=True)

    def placed(k):
        loop(1, n, lambda i: a_copy(k, i, req, other(i)).wait_recv())
        return jnp.dot(arrived[k].T, place[...], preferred_element_type=F32)

    blocks = [slice(b * LANES, (b + 1) * LANES) for b in range(rows // LANES)]

    def u_copy(a):
        return across(u_send.at[a], u_recv.at[a], u_s.at[a], u_r.at[a])

    def merge_late(a):
        c = EARLY + a
        images_t = placed(CHUNKS + a)
        for at in blocks:
            part = jnp.dot(text[at, :], w[0, c], preferred_element_type=F32)
            u_send[a, :, at] = jnp.where(filled[:, at] > 0.5, images_t[:, at], part.T).astype(BF16)
        u_copy(a).start()
        images_t = placed(c)
        for at in blocks:
            u_own[a, :, at] = jnp.where(filled[:, at] > 0.5, images_t[:, at], t_own[c, at, :].T)

    loop(0, LATE, merge_late)
    copy_sq_text.wait()

    def out_copy(c):
        return pltpu.make_async_copy(
            outv.at[c], out_hbm.at[pl.ds(pl.multiple_of(c * cw, cw), cw), :], o_sem.at[c]
        )

    def text_inv(b):
        return lax.rsqrt((sq_text[b] + sq_text_in[b]) / width + EPSILON)

    def finish(c):
        images_t = placed(c)
        t_copy(c).wait_recv()
        for b, at in enumerate(blocks):
            texts = (t_own[c, at, :] + t_recv[c, at, :].astype(F32)).T * text_inv(b)
            outv[c, :, at] = jnp.where(filled[:, at] > 0.5, images_t[:, at], texts).astype(BF16)
        out_copy(c).start()

    loop(0, EARLY, finish)

    def finish_late(a):
        u_copy(a).wait_recv()
        for b, at in enumerate(blocks):
            inv = jnp.where(filled[:, at] > 0.5, 1.0, text_inv(b))
            outv[EARLY + a, :, at] = ((u_own[a, :, at] + u_recv[a, :, at].astype(F32)) * inv).astype(BF16)
        out_copy(EARLY + a).start()

    loop(0, LATE, finish_late)

    loop(1, n, lambda i: pos_copy(i, req).wait_send())
    loop(0, LATE, lambda a: u_copy(a).wait_send())
    loop(0, CHUNKS, lambda c: out_copy(c).wait())

    def drain(c):
        p_copy(c).wait_send()
        t_copy(c).wait_send()

    loop(0, EARLY, drain)
    loop(0, CHUNKS + LATE, lambda k: loop(1, n, lambda i: a_copy(k, i, other(i), req).wait_send()))


def local(text_stream, image_rows, positions, norm_gain, kv_weight):
    n, sides = lax.axis_size("req"), lax.axis_size("tp")
    rows, features = text_stream.shape
    images = image_rows.shape[0]
    half = kv_weight.shape[1] // sides
    cw = half // CHUNKS
    slots = 2 * images
    any_spec, vmem = pl.BlockSpec(memory_space=pl.ANY), pl.BlockSpec(memory_space=pltpu.VMEM)
    dma = pltpu.SemaphoreType.DMA
    return pl.pallas_call(
        functools.partial(kernel, n, features * sides),
        out_shape=jax.ShapeDtypeStruct((half, rows), BF16),
        in_specs=[vmem, vmem, any_spec, any_spec, any_spec],
        out_specs=any_spec,
        scratch_shapes=[
            pltpu.VMEM((images, features), BF16),
            pltpu.VMEM((rows, features), BF16),
            pltpu.VMEM((2, CHUNKS, features, cw), BF16),
            pltpu.VMEM((n, 1, images), jnp.int32),
            pltpu.VMEM((2, n, images), F32),
            pltpu.VMEM((EARLY, images, cw), BF16),
            pltpu.VMEM((EARLY, images, cw), BF16),
            pltpu.VMEM((EARLY, images, cw), F32),
            pltpu.VMEM((EARLY, rows, cw), BF16),
            pltpu.VMEM((EARLY, rows, cw), BF16),
            pltpu.VMEM((CHUNKS, rows, cw), F32),
            pltpu.VMEM((LATE, cw, rows), BF16),
            pltpu.VMEM((LATE, cw, rows), BF16),
            pltpu.VMEM((LATE, cw, rows), F32),
            pltpu.VMEM((images // LANES, 1, LANES), F32),
            pltpu.VMEM((images // LANES, 1, LANES), F32),
            pltpu.VMEM((rows // LANES, 1, LANES), F32),
            pltpu.VMEM((rows // LANES, 1, LANES), F32),
            pltpu.VMEM((images, LANES), F32),
            pltpu.VMEM((slots, images), BF16),
            pltpu.VMEM((CHUNKS + LATE, slots, cw), BF16),
            pltpu.VMEM((CHUNKS + LATE, slots, cw), BF16),
            pltpu.VMEM((slots, rows), BF16),
            pltpu.VMEM((CHUNKS, cw, rows), BF16),
            dma((2,)), dma((2, CHUNKS)), dma((n,)), dma((n,)), dma((2,)), dma((2,)),
            dma((EARLY,)), dma((EARLY,)), dma((EARLY,)), dma((EARLY,)), dma((LATE,)), dma((LATE,)),
            dma((CHUNKS + LATE, n)), dma((CHUNKS + LATE, n)), dma((CHUNKS,)),
        ],
        compiler_params=pltpu.CompilerParams(
            collective_id=0, has_side_effects=True, vmem_limit_bytes=56 * 1024 * 1024
        ),
        cost_estimate=pl.CostEstimate(
            flops=2 * (rows + images) * features * half * sides, bytes_accessed=16 << 20, transcendentals=0
        ),
    )(
        positions.reshape(1, images), norm_gain.reshape(1, features),
        image_rows, text_stream, kv_weight,
    )


def solution(mesh):
    return jax.shard_map(
        local,
        mesh=mesh,
        in_specs=(P("req", "tp"), P("req", "tp"), P("req"), P("tp"), P("tp", None)),
        out_specs=P("tp", "req"),
        check_vma=False,
    )
```

```python
import functools

import jax
import jax.numpy as jnp
from jax import lax
from jax.experimental import pallas as pl
from jax.experimental.pallas import tpu as pltpu
from jax.sharding import PartitionSpec as P

EPSILON = 1e-05
LANES = 128
CHUNKS = 4
LATE = 1
EARLY = CHUNKS - LATE
MESH = pl.DeviceIdType.MESH
F32 = jnp.float32
BF16 = jnp.bfloat16


def iota(shape, dim):
    return lax.broadcasted_iota(jnp.int32, shape, dim)


def loop(start, stop, body):
    def step(i, carry):
        body(i)
        return carry

    lax.fori_loop(start, stop, step, 0)


def squares(x_ref, squares_ref, gain_ref=None):
    def body(b):
        rows = pl.ds(pl.multiple_of(b * LANES, LANES), LANES)
        total = jnp.zeros((LANES, LANES), F32)
        for k in range(x_ref.shape[1] // LANES):
            piece = x_ref[rows, k * LANES:(k + 1) * LANES].astype(F32)
            total = total + piece * piece
        squares_ref[b] = jnp.sum(total.T, axis=0, keepdims=True)
        if gain_ref is not None:
            x_ref[rows, :] = x_ref[rows, :] * gain_ref[...]

    loop(0, x_ref.shape[0] // LANES, body)


def kernel(
    n, width, pos_ref, gain_ref, img_hbm, text_hbm, w_hbm, out_hbm,
    gain, raw, img, text, w, pos_all, rank, p_send, p_recv, p_own, t_send, t_recv, t_own,
    u_send, u_recv, u_own,
    sq_img, sq_img_in, sq_text, sq_text_in, inv_img, pick, pack, arrived, place, outv,
    ld_sem, w_sem, pos_s, pos_r, sq_s, sq_r, p_s, p_r, t_s, t_r, u_s, u_r, a_s, a_r, o_sem,
):
    gain_row = gain_ref[...].reshape(1, gain_ref.shape[0])
    gain[...] = gain_row
    req, tp = lax.axis_index("req"), lax.axis_index("tp")
    peer = 1 - tp
    images, rows = img.shape[0], text.shape[0]
    cw = w.shape[3]
    half = CHUNKS * cw
    slots = place.shape[0]
    cap = slots // n

    def other(i):
        return lax.rem(req + i, n)

    def load_w(side, owner, c):
        return pltpu.make_async_copy(
            w_hbm.at[:, pl.ds(pl.multiple_of(owner * half + c * cw, cw), cw)], w.at[side, c], w_sem.at[side, c]
        )

    load_img = pltpu.make_async_copy(img_hbm, raw, ld_sem.at[0])
    load_text = pltpu.make_async_copy(text_hbm, text, ld_sem.at[1])
    load_img.start()
    load_w(0, peer, 0).start()

    barrier = pltpu.get_barrier_semaphore()
    loop(1, n, lambda i: pl.semaphore_signal(barrier, inc=1, device_id={"req": other(i)}, device_id_type=MESH))
    pl.semaphore_signal(barrier, inc=1, device_id={"tp": peer}, device_id_type=MESH)
    pl.semaphore_wait(barrier, n)

    def across(src, dst, send, recv):
        return pltpu.make_async_remote_copy(
            src_ref=src, dst_ref=dst, send_sem=send, recv_sem=recv, device_id={"tp": peer}, device_id_type=MESH
        )

    def pos_copy(i, source):
        return pltpu.make_async_remote_copy(
            src_ref=pos_all.at[source], dst_ref=pos_all.at[source], send_sem=pos_s.at[i],
            recv_sem=pos_r.at[source], device_id={"req": other(i)}, device_id_type=MESH,
        )

    pos_all[pl.ds(req, 1)] = pos_ref[...].reshape(1, 1, images)
    loop(1, n, lambda i: pos_copy(i, req).start())

    load_img.wait()
    loop(1, CHUNKS, lambda c: load_w(0, peer, c).start())
    load_text.start()
    loop(EARLY, CHUNKS, lambda c: load_w(1, tp, c).start())
    loop(0, EARLY, lambda c: load_w(1, tp, c).start())

    def gain_body(b):
        at = pl.ds(pl.multiple_of(b * LANES, LANES), LANES)
        img[at, :] = raw[at, :] * gain[...]

    loop(0, images // LANES, gain_body)

    def p_copy(c):
        return across(p_send.at[c], p_recv.at[c], p_s.at[c], p_r.at[c])

    def image_send(c):
        load_w(0, peer, c).wait()
        p_send[c] = jnp.dot(img[...], w[0, c], preferred_element_type=F32).astype(BF16)
        p_copy(c).start()

    image_send(0)
    squares(raw, sq_img)
    copy_sq_img = across(sq_img, sq_img_in, sq_s.at[0], sq_r.at[0])
    copy_sq_img.start()
    loop(1, EARLY, image_send)

    row_pos = pos_ref[...]
    dest = iota((n, images), 0)
    member = (row_pos >= dest * rows) & (row_pos < (dest + 1) * rows)
    earlier = (iota((images, images), 0) < iota((images, images), 1)).astype(F32).astype(BF16)
    ones = member.astype(F32)
    before = jnp.dot(ones.astype(BF16), earlier, preferred_element_type=F32)
    target = jnp.sum((before + (dest * cap).astype(F32)) * ones, axis=0, keepdims=True)
    slot = iota((slots, images), 0).astype(F32)
    pick[...] = (slot == target).astype(F32).astype(BF16)

    copy_sq_img.wait()

    def inv_body(b):
        inv = lax.rsqrt((sq_img[b] + sq_img_in[b]) / width + EPSILON)
        inv_img[pl.ds(pl.multiple_of(b * LANES, LANES), LANES), :] = jnp.broadcast_to(inv, (LANES, LANES)).T

    loop(0, images // LANES, inv_body)

    def a_copy(c, i, dst, source):
        return pltpu.make_async_remote_copy(
            src_ref=pack.at[c, pl.ds(pl.multiple_of(dst * cap, cap), cap), :],
            dst_ref=arrived.at[c, pl.ds(pl.multiple_of(source * cap, cap), cap), :],
            send_sem=a_s.at[c, i], recv_sem=a_r.at[c, source],
            device_id={"req": other(i)}, device_id_type=MESH,
        )

    def pack_and_send(k, scaled):
        pack[k] = jnp.dot(pick[...], scaled, preferred_element_type=F32).astype(BF16)
        loop(1, n, lambda i: a_copy(k, i, other(i), req).start())
        mine = pl.ds(pl.multiple_of(req * cap, cap), cap)
        arrived[k, mine, :] = pack[k, mine, :]

    def scale(total):
        inv = inv_img[...]
        return jnp.concatenate(
            [total[:, k * LANES:(k + 1) * LANES] * inv for k in range(cw // LANES)], axis=1
        ).astype(BF16)

    def image_late(side, owner, c, k):
        load_w(side, owner, c).wait()
        pack_and_send(k, scale(jnp.dot(img[...], w[side, c], preferred_element_type=F32)))

    loop(0, LATE, lambda a: image_late(0, peer, EARLY + a, CHUNKS + a))

    load_text.wait()
    squares(text, sq_text, gain)

    def t_copy(c):
        return across(t_send.at[c], t_recv.at[c], t_s.at[c], t_r.at[c])

    def text_send(c):
        t_send[c] = jnp.dot(text[...], w[0, c], preferred_element_type=F32).astype(BF16)

    text_send(0)
    loop(EARLY, CHUNKS, lambda c: image_late(1, tp, c, c))

    def image_own(c):
        load_w(1, tp, c).wait()
        p_own[c] = jnp.dot(img[...], w[1, c], preferred_element_type=F32)

    loop(0, EARLY, image_own)

    copy_sq_text = across(sq_text, sq_text_in, sq_s.at[1], sq_r.at[1])
    copy_sq_text.start()

    def image_pack(c):
        p_copy(c).wait_recv()
        t_copy(c).start()
        pack_and_send(c, scale(p_own[c] + p_recv[c].astype(F32)))

        @pl.when(c + 1 < EARLY)
        def _():
            text_send(c + 1)

    loop(0, EARLY, image_pack)

    loop(1, n, lambda i: pos_copy(i, other(i)).wait_recv())
    all_pos = pos_all[:, 0, :]
    local = all_pos - req * rows
    here = (local >= 0) & (local < rows)
    here_f = here.astype(F32)
    order = jnp.dot(here_f.astype(BF16), earlier, preferred_element_type=F32)
    rank[0] = jnp.where(here, order, -1.0)
    rank[1] = local.astype(F32) + 1.0

    def place_body(g):
        eight = pl.ds(pl.multiple_of(g * 8, 8), 8)
        order8 = rank[0, eight, :]
        local8 = rank[1, eight, :]
        for k in range(8):
            hit = iota((cap, images), 0).astype(F32) == order8[k:k + 1, :]
            at = jnp.sum(jnp.where(hit, local8[k:k + 1, :], 0.0), axis=1, keepdims=True)
            block = (iota((cap, rows), 1).astype(F32) + 1.0) == at
            place[pl.ds(pl.multiple_of((g * 8 + k) * cap, cap), cap), :] = block.astype(F32).astype(BF16)

    loop(0, n // 8, place_body)

    filled = jnp.max(place[...].astype(F32), axis=0, keepdims=True)

    def placed(k):
        loop(1, n, lambda i: a_copy(k, i, req, other(i)).wait_recv())
        return jnp.dot(arrived[k].T, place[...], preferred_element_type=F32)

    blocks = [slice(b * LANES, (b + 1) * LANES) for b in range(rows // LANES)]

    def u_copy(a):
        return across(u_send.at[a], u_recv.at[a], u_s.at[a], u_r.at[a])

    def merge_late(a):
        c = EARLY + a
        images_t = placed(CHUNKS + a)
        for at in blocks:
            part = jnp.dot(text[at, :], w[0, c], preferred_element_type=F32)
            u_send[a, :, at] = jnp.where(filled[:, at] > 0.5, images_t[:, at], part.T).astype(BF16)
        u_copy(a).start()

    loop(0, LATE, merge_late)

    def text_own(c):
        t_own[c] = jnp.dot(text[...], w[1, c], preferred_element_type=F32)

    loop(0, CHUNKS, text_own)

    def own_late(a):
        c = EARLY + a
        images_t = placed(c)
        for at in blocks:
            u_own[a, :, at] = jnp.where(filled[:, at] > 0.5, images_t[:, at], t_own[c, at, :].T)

    copy_sq_text.wait()

    def out_copy(c):
        return pltpu.make_async_copy(
            outv.at[c], out_hbm.at[pl.ds(pl.multiple_of(c * cw, cw), cw), :], o_sem.at[c]
        )

    def text_inv(b):
        return lax.rsqrt((sq_text[b] + sq_text_in[b]) / width + EPSILON)

    def finish_text(c):
        t_copy(c).wait_recv()
        for b, at in enumerate(blocks):
            texts = (t_own[c, at, :] + t_recv[c, at, :].astype(F32)).T * text_inv(b)
            outv[c, :, at] = texts.astype(BF16)

    def finish_images(c):
        images_t = placed(c)
        outv[c] = jnp.where(filled > 0.5, images_t, outv[c].astype(F32)).astype(BF16)
        out_copy(c).start()

    loop(0, EARLY, finish_text)
    loop(0, LATE, own_late)
    loop(0, EARLY, finish_images)

    def finish_late(a):
        u_copy(a).wait_recv()
        for b, at in enumerate(blocks):
            inv = jnp.where(filled[:, at] > 0.5, 1.0, text_inv(b))
            outv[EARLY + a, :, at] = ((u_own[a, :, at] + u_recv[a, :, at].astype(F32)) * inv).astype(BF16)
        out_copy(EARLY + a).start()

    loop(0, LATE, finish_late)

    loop(1, n, lambda i: pos_copy(i, req).wait_send())
    loop(0, LATE, lambda a: u_copy(a).wait_send())
    loop(0, CHUNKS, lambda c: out_copy(c).wait())

    def drain(c):
        p_copy(c).wait_send()
        t_copy(c).wait_send()

    loop(0, EARLY, drain)
    loop(0, CHUNKS + LATE, lambda k: loop(1, n, lambda i: a_copy(k, i, other(i), req).wait_send()))


def local(text_stream, image_rows, positions, norm_gain, kv_weight):
    n, sides = lax.axis_size("req"), lax.axis_size("tp")
    rows, features = text_stream.shape
    images = image_rows.shape[0]
    half = kv_weight.shape[1] // sides
    cw = half // CHUNKS
    slots = 2 * images
    any_spec, vmem = pl.BlockSpec(memory_space=pl.ANY), pl.BlockSpec(memory_space=pltpu.VMEM)
    dma = pltpu.SemaphoreType.DMA
    return pl.pallas_call(
        functools.partial(kernel, n, features * sides),
        out_shape=jax.ShapeDtypeStruct((half, rows), BF16),
        in_specs=[vmem, vmem, any_spec, any_spec, any_spec],
        out_specs=any_spec,
        scratch_shapes=[
            pltpu.VMEM((1, features), BF16),
            pltpu.VMEM((images, features), BF16),
            pltpu.VMEM((images, features), BF16),
            pltpu.VMEM((rows, features), BF16),
            pltpu.VMEM((2, CHUNKS, features, cw), BF16),
            pltpu.VMEM((n, 1, images), jnp.int32),
            pltpu.VMEM((2, n, images), F32),
            pltpu.VMEM((EARLY, images, cw), BF16),
            pltpu.VMEM((EARLY, images, cw), BF16),
            pltpu.VMEM((EARLY, images, cw), F32),
            pltpu.VMEM((EARLY, rows, cw), BF16),
            pltpu.VMEM((EARLY, rows, cw), BF16),
            pltpu.VMEM((CHUNKS, rows, cw), F32),
            pltpu.VMEM((LATE, cw, rows), BF16),
            pltpu.VMEM((LATE, cw, rows), BF16),
            pltpu.VMEM((LATE, cw, rows), F32),
            pltpu.VMEM((images // LANES, 1, LANES), F32),
            pltpu.VMEM((images // LANES, 1, LANES), F32),
            pltpu.VMEM((rows // LANES, 1, LANES), F32),
            pltpu.VMEM((rows // LANES, 1, LANES), F32),
            pltpu.VMEM((images, LANES), F32),
            pltpu.VMEM((slots, images), BF16),
            pltpu.VMEM((CHUNKS + LATE, slots, cw), BF16),
            pltpu.VMEM((CHUNKS + LATE, slots, cw), BF16),
            pltpu.VMEM((slots, rows), BF16),
            pltpu.VMEM((CHUNKS, cw, rows), BF16),
            dma((2,)), dma((2, CHUNKS)), dma((n,)), dma((n,)), dma((2,)), dma((2,)),
            dma((EARLY,)), dma((EARLY,)), dma((EARLY,)), dma((EARLY,)), dma((LATE,)), dma((LATE,)),
            dma((CHUNKS + LATE, n)), dma((CHUNKS + LATE, n)), dma((CHUNKS,)),
        ],
        compiler_params=pltpu.CompilerParams(
            collective_id=0, has_side_effects=True, vmem_limit_bytes=56 * 1024 * 1024
        ),
        cost_estimate=pl.CostEstimate(
            flops=2 * (rows + images) * features * half * sides, bytes_accessed=16 << 20, transcendentals=0
        ),
    )(
        positions.reshape(1, images), norm_gain,
        image_rows, text_stream, kv_weight,
    )


def solution(mesh):
    return jax.shard_map(
        local,
        mesh=mesh,
        in_specs=(P("req", "tp"), P("req", "tp"), P("req"), P("tp"), P("tp", None)),
        out_specs=P("tp", "req"),
        check_vma=False,
    )
```

```python
import functools

import jax
import jax.numpy as jnp
from jax import lax
from jax.experimental import pallas as pl
from jax.experimental.pallas import tpu as pltpu
from jax.sharding import PartitionSpec as P

EPSILON = 1e-05
LANES = 128
CHUNKS = 4
LATE = 1
EARLY = CHUNKS - LATE
MESH = pl.DeviceIdType.MESH
F32 = jnp.float32
BF16 = jnp.bfloat16


def iota(shape, dim):
    return lax.broadcasted_iota(jnp.int32, shape, dim)


def loop(start, stop, body):
    def step(i, carry):
        body(i)
        return carry

    lax.fori_loop(start, stop, step, 0)


def squares(x_ref, squares_ref):
    def body(b):
        rows = pl.ds(pl.multiple_of(b * LANES, LANES), LANES)
        total = jnp.zeros((LANES, LANES), F32)
        for k in range(x_ref.shape[1] // LANES):
            piece = x_ref[rows, k * LANES:(k + 1) * LANES].astype(F32)
            total = total + piece * piece
        squares_ref[b] = jnp.sum(total.T, axis=0, keepdims=True)

    loop(0, x_ref.shape[0] // LANES, body)


def gained(x_ref, gain_ref, out_ref):
    def body(b):
        at = pl.ds(pl.multiple_of(b * LANES, LANES), LANES)
        out_ref[at, :] = x_ref[at, :] * gain_ref[...]

    loop(0, x_ref.shape[0] // LANES, body)


def kernel(
    n, width, pos_ref, gain_ref, img_hbm, text_hbm, w_hbm, out_hbm,
    gain, raw, img, raw_text, text, w, pos_all, rank, p_send, p_recv, p_own, t_send, t_recv, t_own,
    u_send, u_recv, u_own,
    sq_img, sq_img_in, sq_text, sq_text_in, inv_img, pick, pack, arrived, place, outv,
    ld_sem, w_sem, pos_s, pos_r, sq_s, sq_r, p_s, p_r, t_s, t_r, u_s, u_r, a_s, a_r, o_sem,
):
    gain_row = gain_ref[...].reshape(1, gain_ref.shape[0])
    gain[...] = gain_row
    req, tp = lax.axis_index("req"), lax.axis_index("tp")
    peer = 1 - tp
    images, rows = img.shape[0], text.shape[0]
    cw = w.shape[3]
    half = CHUNKS * cw
    slots = place.shape[0]
    cap = slots // n

    def other(i):
        return lax.rem(req + i, n)

    def load_w(side, owner, c):
        return pltpu.make_async_copy(
            w_hbm.at[:, pl.ds(pl.multiple_of(owner * half + c * cw, cw), cw)], w.at[side, c], w_sem.at[side, c]
        )

    load_img = pltpu.make_async_copy(img_hbm, raw, ld_sem.at[0])
    load_text = pltpu.make_async_copy(text_hbm, raw_text, ld_sem.at[1])
    load_img.start()
    load_w(0, peer, 0).start()

    barrier = pltpu.get_barrier_semaphore()
    loop(1, n, lambda i: pl.semaphore_signal(barrier, inc=1, device_id={"req": other(i)}, device_id_type=MESH))
    pl.semaphore_signal(barrier, inc=1, device_id={"tp": peer}, device_id_type=MESH)
    pl.semaphore_wait(barrier, n)

    def across(src, dst, send, recv):
        return pltpu.make_async_remote_copy(
            src_ref=src, dst_ref=dst, send_sem=send, recv_sem=recv, device_id={"tp": peer}, device_id_type=MESH
        )

    def pos_copy(i, source):
        return pltpu.make_async_remote_copy(
            src_ref=pos_all.at[source], dst_ref=pos_all.at[source], send_sem=pos_s.at[i],
            recv_sem=pos_r.at[source], device_id={"req": other(i)}, device_id_type=MESH,
        )

    pos_all[pl.ds(req, 1)] = pos_ref[...].reshape(1, 1, images)
    loop(1, n, lambda i: pos_copy(i, req).start())

    load_img.wait()
    loop(1, CHUNKS, lambda c: load_w(0, peer, c).start())
    load_text.start()
    loop(EARLY, CHUNKS, lambda c: load_w(1, tp, c).start())
    loop(0, EARLY, lambda c: load_w(1, tp, c).start())

    gained(raw, gain, img)

    def p_copy(c):
        return across(p_send.at[c], p_recv.at[c], p_s.at[c], p_r.at[c])

    def image_send(c):
        load_w(0, peer, c).wait()
        p_send[c] = jnp.dot(img[...], w[0, c], preferred_element_type=F32).astype(BF16)
        p_copy(c).start()

    image_send(0)
    squares(raw, sq_img)
    copy_sq_img = across(sq_img, sq_img_in, sq_s.at[0], sq_r.at[0])
    copy_sq_img.start()
    loop(1, EARLY, image_send)

    row_pos = pos_ref[...]
    dest = iota((n, images), 0)
    member = (row_pos >= dest * rows) & (row_pos < (dest + 1) * rows)
    earlier = (iota((images, images), 0) < iota((images, images), 1)).astype(F32).astype(BF16)
    ones = member.astype(F32)
    before = jnp.dot(ones.astype(BF16), earlier, preferred_element_type=F32)
    target = jnp.sum((before + (dest * cap).astype(F32)) * ones, axis=0, keepdims=True)
    slot = iota((slots, images), 0).astype(F32)
    pick[...] = (slot == target).astype(F32).astype(BF16)

    copy_sq_img.wait()

    def inv_body(b):
        inv = lax.rsqrt((sq_img[b] + sq_img_in[b]) / width + EPSILON)
        inv_img[pl.ds(pl.multiple_of(b * LANES, LANES), LANES), :] = jnp.broadcast_to(inv, (LANES, LANES)).T

    loop(0, images // LANES, inv_body)

    def a_copy(c, i, dst, source):
        return pltpu.make_async_remote_copy(
            src_ref=pack.at[c, pl.ds(pl.multiple_of(dst * cap, cap), cap), :],
            dst_ref=arrived.at[c, pl.ds(pl.multiple_of(source * cap, cap), cap), :],
            send_sem=a_s.at[c, i], recv_sem=a_r.at[c, source],
            device_id={"req": other(i)}, device_id_type=MESH,
        )

    def pack_and_send(k, scaled):
        pack[k] = jnp.dot(pick[...], scaled, preferred_element_type=F32).astype(BF16)
        loop(1, n, lambda i: a_copy(k, i, other(i), req).start())
        mine = pl.ds(pl.multiple_of(req * cap, cap), cap)
        arrived[k, mine, :] = pack[k, mine, :]

    def scale(total):
        inv = inv_img[...]
        return jnp.concatenate(
            [total[:, k * LANES:(k + 1) * LANES] * inv for k in range(cw // LANES)], axis=1
        ).astype(BF16)

    def image_late(side, owner, c, k):
        load_w(side, owner, c).wait()
        pack_and_send(k, scale(jnp.dot(img[...], w[side, c], preferred_element_type=F32)))

    loop(0, LATE, lambda a: image_late(0, peer, EARLY + a, CHUNKS + a))
    loop(EARLY, CHUNKS, lambda c: image_late(1, tp, c, c))

    load_text.wait()
    gained(raw_text, gain, text)

    def t_copy(c):
        return across(t_send.at[c], t_recv.at[c], t_s.at[c], t_r.at[c])

    def text_send(c):
        t_send[c] = jnp.dot(text[...], w[0, c], preferred_element_type=F32).astype(BF16)
        t_copy(c).start()

    text_send(0)
    def image_own(c):
        load_w(1, tp, c).wait()
        p_own[c] = jnp.dot(img[...], w[1, c], preferred_element_type=F32)

    loop(0, EARLY, image_own)

    def image_pack(c):
        p_copy(c).wait_recv()
        pack_and_send(c, scale(p_own[c] + p_recv[c].astype(F32)))

        @pl.when(c + 1 < EARLY)
        def _():
            text_send(c + 1)

    loop(0, EARLY, image_pack)

    loop(1, n, lambda i: pos_copy(i, other(i)).wait_recv())
    all_pos = pos_all[:, 0, :]
    local = all_pos - req * rows
    here = (local >= 0) & (local < rows)
    here_f = here.astype(F32)
    order = jnp.dot(here_f.astype(BF16), earlier, preferred_element_type=F32)
    rank[0] = jnp.where(here, order, -1.0)
    rank[1] = local.astype(F32) + 1.0

    def place_body(g):
        eight = pl.ds(pl.multiple_of(g * 8, 8), 8)
        order8 = rank[0, eight, :]
        local8 = rank[1, eight, :]
        for k in range(8):
            hit = iota((cap, images), 0).astype(F32) == order8[k:k + 1, :]
            at = jnp.sum(jnp.where(hit, local8[k:k + 1, :], 0.0), axis=1, keepdims=True)
            block = (iota((cap, rows), 1).astype(F32) + 1.0) == at
            place[pl.ds(pl.multiple_of((g * 8 + k) * cap, cap), cap), :] = block.astype(F32).astype(BF16)

    loop(0, n // 8, place_body)

    filled = jnp.max(place[...].astype(F32), axis=0, keepdims=True)

    def placed(k):
        loop(1, n, lambda i: a_copy(k, i, req, other(i)).wait_recv())
        return jnp.dot(arrived[k].T, place[...], preferred_element_type=F32)

    blocks = [slice(b * LANES, (b + 1) * LANES) for b in range(rows // LANES)]

    def u_copy(a):
        return across(u_send.at[a], u_recv.at[a], u_s.at[a], u_r.at[a])

    def merge_late(a):
        c = EARLY + a
        t_own[c] = jnp.dot(text[...], w[0, c], preferred_element_type=F32)
        images_t = placed(CHUNKS + a)
        for at in blocks:
            u_send[a, :, at] = jnp.where(filled[:, at] > 0.5, images_t[:, at], t_own[c, at, :].T).astype(BF16)
        u_copy(a).start()

    loop(0, LATE, merge_late)
    squares(raw_text, sq_text)
    copy_sq_text = across(sq_text, sq_text_in, sq_s.at[1], sq_r.at[1])
    copy_sq_text.start()

    def text_own(c):
        t_own[c] = jnp.dot(text[...], w[1, c], preferred_element_type=F32)

    loop(0, CHUNKS, text_own)

    def own_late(a):
        c = EARLY + a
        images_t = placed(c)
        for at in blocks:
            u_own[a, :, at] = jnp.where(filled[:, at] > 0.5, images_t[:, at], t_own[c, at, :].T)

    copy_sq_text.wait()

    def out_copy(c):
        return pltpu.make_async_copy(
            outv.at[c], out_hbm.at[pl.ds(pl.multiple_of(c * cw, cw), cw), :], o_sem.at[c]
        )

    def text_inv(b):
        return lax.rsqrt((sq_text[b] + sq_text_in[b]) / width + EPSILON)

    def finish_text(c):
        t_copy(c).wait_recv()
        for b, at in enumerate(blocks):
            texts = (t_own[c, at, :] + t_recv[c, at, :].astype(F32)).T * text_inv(b)
            outv[c, :, at] = texts.astype(BF16)

    def finish_images(c):
        images_t = placed(c)
        outv[c] = jnp.where(filled > 0.5, images_t, outv[c].astype(F32)).astype(BF16)
        out_copy(c).start()

    loop(0, EARLY, finish_text)
    loop(0, LATE, own_late)
    loop(0, EARLY, finish_images)

    def finish_late(a):
        u_copy(a).wait_recv()
        for b, at in enumerate(blocks):
            inv = jnp.where(filled[:, at] > 0.5, 1.0, text_inv(b))
            outv[EARLY + a, :, at] = ((u_own[a, :, at] + u_recv[a, :, at].astype(F32)) * inv).astype(BF16)
        out_copy(EARLY + a).start()

    loop(0, LATE, finish_late)

    loop(1, n, lambda i: pos_copy(i, req).wait_send())
    loop(0, LATE, lambda a: u_copy(a).wait_send())
    loop(0, CHUNKS, lambda c: out_copy(c).wait())

    def drain(c):
        p_copy(c).wait_send()
        t_copy(c).wait_send()

    loop(0, EARLY, drain)
    loop(0, CHUNKS + LATE, lambda k: loop(1, n, lambda i: a_copy(k, i, other(i), req).wait_send()))


def local(text_stream, image_rows, positions, norm_gain, kv_weight):
    n, sides = lax.axis_size("req"), lax.axis_size("tp")
    rows, features = text_stream.shape
    images = image_rows.shape[0]
    half = kv_weight.shape[1] // sides
    cw = half // CHUNKS
    slots = 2 * images
    any_spec, vmem = pl.BlockSpec(memory_space=pl.ANY), pl.BlockSpec(memory_space=pltpu.VMEM)
    dma = pltpu.SemaphoreType.DMA
    return pl.pallas_call(
        functools.partial(kernel, n, features * sides),
        out_shape=jax.ShapeDtypeStruct((half, rows), BF16),
        in_specs=[vmem, vmem, any_spec, any_spec, any_spec],
        out_specs=any_spec,
        scratch_shapes=[
            pltpu.VMEM((1, features), BF16),
            pltpu.VMEM((images, features), BF16),
            pltpu.VMEM((images, features), BF16),
            pltpu.VMEM((rows, features), BF16),
            pltpu.VMEM((rows, features), BF16),
            pltpu.VMEM((2, CHUNKS, features, cw), BF16),
            pltpu.VMEM((n, 1, images), jnp.int32),
            pltpu.VMEM((2, n, images), F32),
            pltpu.VMEM((EARLY, images, cw), BF16),
            pltpu.VMEM((EARLY, images, cw), BF16),
            pltpu.VMEM((EARLY, images, cw), F32),
            pltpu.VMEM((EARLY, rows, cw), BF16),
            pltpu.VMEM((EARLY, rows, cw), BF16),
            pltpu.VMEM((CHUNKS, rows, cw), F32),
            pltpu.VMEM((LATE, cw, rows), BF16),
            pltpu.VMEM((LATE, cw, rows), BF16),
            pltpu.VMEM((LATE, cw, rows), F32),
            pltpu.VMEM((images // LANES, 1, LANES), F32),
            pltpu.VMEM((images // LANES, 1, LANES), F32),
            pltpu.VMEM((rows // LANES, 1, LANES), F32),
            pltpu.VMEM((rows // LANES, 1, LANES), F32),
            pltpu.VMEM((images, LANES), F32),
            pltpu.VMEM((slots, images), BF16),
            pltpu.VMEM((CHUNKS + LATE, slots, cw), BF16),
            pltpu.VMEM((CHUNKS + LATE, slots, cw), BF16),
            pltpu.VMEM((slots, rows), BF16),
            pltpu.VMEM((CHUNKS, cw, rows), BF16),
            dma((2,)), dma((2, CHUNKS)), dma((n,)), dma((n,)), dma((2,)), dma((2,)),
            dma((EARLY,)), dma((EARLY,)), dma((EARLY,)), dma((EARLY,)), dma((LATE,)), dma((LATE,)),
            dma((CHUNKS + LATE, n)), dma((CHUNKS + LATE, n)), dma((CHUNKS,)),
        ],
        compiler_params=pltpu.CompilerParams(
            collective_id=0, has_side_effects=True, vmem_limit_bytes=56 * 1024 * 1024
        ),
        cost_estimate=pl.CostEstimate(
            flops=2 * (rows + images) * features * half * sides, bytes_accessed=16 << 20, transcendentals=0
        ),
    )(
        positions.reshape(1, images), norm_gain,
        image_rows, text_stream, kv_weight,
    )


def solution(mesh):
    return jax.shard_map(
        local,
        mesh=mesh,
        in_specs=(P("req", "tp"), P("req", "tp"), P("req"), P("tp"), P("tp", None)),
        out_specs=P("tp", "req"),
        check_vma=False,
    )
```

```python
import functools

import jax
import jax.numpy as jnp
from jax import lax
from jax.experimental import pallas as pl
from jax.experimental.pallas import tpu as pltpu
from jax.sharding import PartitionSpec as P

EPSILON = 1e-05
LANES = 128
CHUNKS = 4
LATE = 1
EARLY = CHUNKS - LATE
MESH = pl.DeviceIdType.MESH
F32 = jnp.float32
BF16 = jnp.bfloat16


def iota(shape, dim):
    return lax.broadcasted_iota(jnp.int32, shape, dim)


def loop(start, stop, body):
    def step(i, carry):
        body(i)
        return carry

    lax.fori_loop(start, stop, step, 0)


def squares(x_ref, squares_ref):
    def body(b):
        rows = pl.ds(pl.multiple_of(b * LANES, LANES), LANES)
        total = jnp.zeros((LANES, LANES), F32)
        for k in range(x_ref.shape[1] // LANES):
            piece = x_ref[rows, k * LANES:(k + 1) * LANES].astype(F32)
            total = total + piece * piece
        squares_ref[b] = jnp.sum(total.T, axis=0, keepdims=True)

    loop(0, x_ref.shape[0] // LANES, body)


def gained(x_ref, gain_ref, out_ref):
    def body(b):
        at = pl.ds(pl.multiple_of(b * LANES, LANES), LANES)
        out_ref[at, :] = x_ref[at, :] * gain_ref[...]

    loop(0, x_ref.shape[0] // LANES, body)


def kernel(
    n, width, pos_ref, gain_ref, img_hbm, text_hbm, w_hbm, out_hbm,
    gain, raw, img, raw_text, text, w, pos_all, rank, p_send, p_recv, p_own, t_send, t_recv, t_own,
    u_send, u_recv, u_own,
    sq_img, sq_img_in, sq_text, sq_text_in, inv_img, pick, pack, arrived, place, outv,
    ld_sem, w_sem, pos_s, pos_r, sq_s, sq_r, p_s, p_r, t_s, t_r, u_s, u_r, a_s, a_r, o_sem,
):
    gain_row = gain_ref[...].reshape(1, gain_ref.shape[0])
    gain[...] = gain_row
    req, tp = lax.axis_index("req"), lax.axis_index("tp")
    peer = 1 - tp
    images, rows = img.shape[0], text.shape[0]
    cw = w.shape[3]
    half = CHUNKS * cw
    slots = place.shape[0]
    cap = slots // n

    def other(i):
        return lax.rem(req + i, n)

    def load_w(side, owner, c):
        return pltpu.make_async_copy(
            w_hbm.at[:, pl.ds(pl.multiple_of(owner * half + c * cw, cw), cw)], w.at[side, c], w_sem.at[side, c]
        )

    load_img = pltpu.make_async_copy(img_hbm, raw, ld_sem.at[0])
    load_text = pltpu.make_async_copy(text_hbm, raw_text, ld_sem.at[1])
    load_img.start()
    load_w(0, peer, 0).start()

    barrier = pltpu.get_barrier_semaphore()
    loop(1, n, lambda i: pl.semaphore_signal(barrier, inc=1, device_id={"req": other(i)}, device_id_type=MESH))
    pl.semaphore_signal(barrier, inc=1, device_id={"tp": peer}, device_id_type=MESH)
    pl.semaphore_wait(barrier, n)

    def across(src, dst, send, recv):
        return pltpu.make_async_remote_copy(
            src_ref=src, dst_ref=dst, send_sem=send, recv_sem=recv, device_id={"tp": peer}, device_id_type=MESH
        )

    def pos_copy(i, source):
        return pltpu.make_async_remote_copy(
            src_ref=pos_all.at[source], dst_ref=pos_all.at[source], send_sem=pos_s.at[i],
            recv_sem=pos_r.at[source], device_id={"req": other(i)}, device_id_type=MESH,
        )

    pos_all[pl.ds(req, 1)] = pos_ref[...].reshape(1, 1, images)
    loop(1, n, lambda i: pos_copy(i, req).start())

    load_img.wait()
    loop(1, CHUNKS, lambda c: load_w(0, peer, c).start())
    load_text.start()
    loop(EARLY, CHUNKS, lambda c: load_w(1, tp, c).start())
    loop(0, EARLY, lambda c: load_w(1, tp, c).start())

    gained(raw, gain, img)

    def p_copy(c):
        return across(p_send.at[c], p_recv.at[c], p_s.at[c], p_r.at[c])

    def image_send(c):
        load_w(0, peer, c).wait()
        p_send[c] = jnp.dot(img[...], w[0, c], preferred_element_type=F32).astype(BF16)
        p_copy(c).start()

    image_send(0)
    squares(raw, sq_img)
    copy_sq_img = across(sq_img, sq_img_in, sq_s.at[0], sq_r.at[0])
    copy_sq_img.start()
    loop(1, EARLY, image_send)

    row_pos = pos_ref[...]
    dest = iota((n, images), 0)
    member = (row_pos >= dest * rows) & (row_pos < (dest + 1) * rows)
    earlier = (iota((images, images), 0) < iota((images, images), 1)).astype(F32).astype(BF16)
    ones = member.astype(F32)
    before = jnp.dot(ones.astype(BF16), earlier, preferred_element_type=F32)
    target = jnp.sum((before + (dest * cap).astype(F32)) * ones, axis=0, keepdims=True)
    slot = iota((slots, images), 0).astype(F32)
    pick[...] = (slot == target).astype(F32).astype(BF16)

    copy_sq_img.wait()

    def inv_body(b):
        inv = lax.rsqrt((sq_img[b] + sq_img_in[b]) / width + EPSILON)
        inv_img[pl.ds(pl.multiple_of(b * LANES, LANES), LANES), :] = jnp.broadcast_to(inv, (LANES, LANES)).T

    loop(0, images // LANES, inv_body)

    def a_copy(c, i, dst, source):
        return pltpu.make_async_remote_copy(
            src_ref=pack.at[c, pl.ds(pl.multiple_of(dst * cap, cap), cap), :],
            dst_ref=arrived.at[c, pl.ds(pl.multiple_of(source * cap, cap), cap), :],
            send_sem=a_s.at[c, i], recv_sem=a_r.at[c, source],
            device_id={"req": other(i)}, device_id_type=MESH,
        )

    def pack_and_send(k, scaled):
        pack[k] = jnp.dot(pick[...], scaled, preferred_element_type=F32).astype(BF16)
        loop(1, n, lambda i: a_copy(k, i, other(i), req).start())
        mine = pl.ds(pl.multiple_of(req * cap, cap), cap)
        arrived[k, mine, :] = pack[k, mine, :]

    def scale(total):
        inv = inv_img[...]
        return jnp.concatenate(
            [total[:, k * LANES:(k + 1) * LANES] * inv for k in range(cw // LANES)], axis=1
        ).astype(BF16)

    def image_late(side, owner, c, k):
        load_w(side, owner, c).wait()
        pack_and_send(k, scale(jnp.dot(img[...], w[side, c], preferred_element_type=F32)))

    loop(0, LATE, lambda a: image_late(0, peer, EARLY + a, CHUNKS + a))
    loop(EARLY, CHUNKS, lambda c: image_late(1, tp, c, c))

    load_text.wait()
    gained(raw_text, gain, text)

    def t_copy(c):
        return across(t_send.at[c], t_recv.at[c], t_s.at[c], t_r.at[c])

    def text_send(c):
        t_send[c] = jnp.dot(text[...], w[0, c], preferred_element_type=F32).astype(BF16)
    def image_own(c):
        load_w(1, tp, c).wait()
        p_own[c] = jnp.dot(img[...], w[1, c], preferred_element_type=F32)

    loop(0, EARLY, image_own)
    text_send(0)

    def image_pack(c):
        p_copy(c).wait_recv()

        @pl.when(c == EARLY - 1)
        def _():
            t_copy(0).start()

        pack_and_send(c, scale(p_own[c] + p_recv[c].astype(F32)))

    def text_rest(c):
        text_send(c)
        t_copy(c).start()

    loop(0, EARLY, image_pack)
    loop(1, EARLY, text_rest)

    loop(1, n, lambda i: pos_copy(i, other(i)).wait_recv())
    all_pos = pos_all[:, 0, :]
    local = all_pos - req * rows
    here = (local >= 0) & (local < rows)
    here_f = here.astype(F32)
    order = jnp.dot(here_f.astype(BF16), earlier, preferred_element_type=F32)
    rank[0] = jnp.where(here, order, -1.0)
    rank[1] = local.astype(F32) + 1.0

    def place_body(g):
        eight = pl.ds(pl.multiple_of(g * 8, 8), 8)
        order8 = rank[0, eight, :]
        local8 = rank[1, eight, :]
        for k in range(8):
            hit = iota((cap, images), 0).astype(F32) == order8[k:k + 1, :]
            at = jnp.sum(jnp.where(hit, local8[k:k + 1, :], 0.0), axis=1, keepdims=True)
            block = (iota((cap, rows), 1).astype(F32) + 1.0) == at
            place[pl.ds(pl.multiple_of((g * 8 + k) * cap, cap), cap), :] = block.astype(F32).astype(BF16)

    loop(0, n // 8, place_body)

    filled = jnp.max(place[...].astype(F32), axis=0, keepdims=True)

    def placed(k):
        loop(1, n, lambda i: a_copy(k, i, req, other(i)).wait_recv())
        return jnp.dot(arrived[k].T, place[...], preferred_element_type=F32)

    blocks = [slice(b * LANES, (b + 1) * LANES) for b in range(rows // LANES)]

    def u_copy(a):
        return across(u_send.at[a], u_recv.at[a], u_s.at[a], u_r.at[a])

    def merge_late(a):
        c = EARLY + a
        t_own[c] = jnp.dot(text[...], w[0, c], preferred_element_type=F32)
        images_t = placed(CHUNKS + a)
        for at in blocks:
            u_send[a, :, at] = jnp.where(filled[:, at] > 0.5, images_t[:, at], t_own[c, at, :].T).astype(BF16)
        u_copy(a).start()

    loop(0, LATE, merge_late)
    squares(raw_text, sq_text)
    copy_sq_text = across(sq_text, sq_text_in, sq_s.at[1], sq_r.at[1])
    copy_sq_text.start()

    def text_own(c):
        t_own[c] = jnp.dot(text[...], w[1, c], preferred_element_type=F32)

    loop(0, CHUNKS, text_own)

    def own_late(a):
        c = EARLY + a
        images_t = placed(c)
        for at in blocks:
            u_own[a, :, at] = jnp.where(filled[:, at] > 0.5, images_t[:, at], t_own[c, at, :].T)

    copy_sq_text.wait()

    def out_copy(c):
        return pltpu.make_async_copy(
            outv.at[c], out_hbm.at[pl.ds(pl.multiple_of(c * cw, cw), cw), :], o_sem.at[c]
        )

    def text_inv(b):
        return lax.rsqrt((sq_text[b] + sq_text_in[b]) / width + EPSILON)

    def finish_text(c):
        t_copy(c).wait_recv()
        for b, at in enumerate(blocks):
            texts = (t_own[c, at, :] + t_recv[c, at, :].astype(F32)).T * text_inv(b)
            outv[c, :, at] = texts.astype(BF16)

    def finish_images(c):
        images_t = placed(c)
        outv[c] = jnp.where(filled > 0.5, images_t, outv[c].astype(F32)).astype(BF16)
        out_copy(c).start()

    loop(0, EARLY, finish_text)
    loop(0, LATE, own_late)
    loop(0, EARLY, finish_images)

    def finish_late(a):
        u_copy(a).wait_recv()
        for b, at in enumerate(blocks):
            inv = jnp.where(filled[:, at] > 0.5, 1.0, text_inv(b))
            outv[EARLY + a, :, at] = ((u_own[a, :, at] + u_recv[a, :, at].astype(F32)) * inv).astype(BF16)
        out_copy(EARLY + a).start()

    loop(0, LATE, finish_late)

    loop(1, n, lambda i: pos_copy(i, req).wait_send())
    loop(0, LATE, lambda a: u_copy(a).wait_send())
    loop(0, CHUNKS, lambda c: out_copy(c).wait())

    def drain(c):
        p_copy(c).wait_send()
        t_copy(c).wait_send()

    loop(0, EARLY, drain)
    loop(0, CHUNKS + LATE, lambda k: loop(1, n, lambda i: a_copy(k, i, other(i), req).wait_send()))


def local(text_stream, image_rows, positions, norm_gain, kv_weight):
    n, sides = lax.axis_size("req"), lax.axis_size("tp")
    rows, features = text_stream.shape
    images = image_rows.shape[0]
    half = kv_weight.shape[1] // sides
    cw = half // CHUNKS
    slots = 2 * images
    any_spec, vmem = pl.BlockSpec(memory_space=pl.ANY), pl.BlockSpec(memory_space=pltpu.VMEM)
    dma = pltpu.SemaphoreType.DMA
    return pl.pallas_call(
        functools.partial(kernel, n, features * sides),
        out_shape=jax.ShapeDtypeStruct((half, rows), BF16),
        in_specs=[vmem, vmem, any_spec, any_spec, any_spec],
        out_specs=any_spec,
        scratch_shapes=[
            pltpu.VMEM((1, features), BF16),
            pltpu.VMEM((images, features), BF16),
            pltpu.VMEM((images, features), BF16),
            pltpu.VMEM((rows, features), BF16),
            pltpu.VMEM((rows, features), BF16),
            pltpu.VMEM((2, CHUNKS, features, cw), BF16),
            pltpu.VMEM((n, 1, images), jnp.int32),
            pltpu.VMEM((2, n, images), F32),
            pltpu.VMEM((EARLY, images, cw), BF16),
            pltpu.VMEM((EARLY, images, cw), BF16),
            pltpu.VMEM((EARLY, images, cw), F32),
            pltpu.VMEM((EARLY, rows, cw), BF16),
            pltpu.VMEM((EARLY, rows, cw), BF16),
            pltpu.VMEM((CHUNKS, rows, cw), F32),
            pltpu.VMEM((LATE, cw, rows), BF16),
            pltpu.VMEM((LATE, cw, rows), BF16),
            pltpu.VMEM((LATE, cw, rows), F32),
            pltpu.VMEM((images // LANES, 1, LANES), F32),
            pltpu.VMEM((images // LANES, 1, LANES), F32),
            pltpu.VMEM((rows // LANES, 1, LANES), F32),
            pltpu.VMEM((rows // LANES, 1, LANES), F32),
            pltpu.VMEM((images, LANES), F32),
            pltpu.VMEM((slots, images), BF16),
            pltpu.VMEM((CHUNKS + LATE, slots, cw), BF16),
            pltpu.VMEM((CHUNKS + LATE, slots, cw), BF16),
            pltpu.VMEM((slots, rows), BF16),
            pltpu.VMEM((CHUNKS, cw, rows), BF16),
            dma((2,)), dma((2, CHUNKS)), dma((n,)), dma((n,)), dma((2,)), dma((2,)),
            dma((EARLY,)), dma((EARLY,)), dma((EARLY,)), dma((EARLY,)), dma((LATE,)), dma((LATE,)),
            dma((CHUNKS + LATE, n)), dma((CHUNKS + LATE, n)), dma((CHUNKS,)),
        ],
        compiler_params=pltpu.CompilerParams(
            collective_id=0, has_side_effects=True, vmem_limit_bytes=56 * 1024 * 1024
        ),
        cost_estimate=pl.CostEstimate(
            flops=2 * (rows + images) * features * half * sides, bytes_accessed=16 << 20, transcendentals=0
        ),
    )(
        positions.reshape(1, images), norm_gain,
        image_rows, text_stream, kv_weight,
    )


def solution(mesh):
    return jax.shard_map(
        local,
        mesh=mesh,
        in_specs=(P("req", "tp"), P("req", "tp"), P("req"), P("tp"), P("tp", None)),
        out_specs=P("tp", "req"),
        check_vma=False,
    )
```
